512 devices in a mesh: pipe: 8 (over y), seq: 8 (over x, core), dp: 8 (over z).
Axes of the slice: x: 4, y: 8, z: 8, core: 2. Of those that a mesh axis runs over, the one named last changes fastest.
Arguments:
- incoming: bfloat16 [8, 3, 8, 1024, 1536], P('pipe', None, 'dp', 'seq'), may hold values from -9 to 9, as said below
- contacts: int32 [10, 8, 1024], P(None, 'dp', 'seq'), may hold values from 0 to 15
- keyframes: int32 [10, 8, 1024], P(None, 'dp'), may hold values 0 or 1
- timesteps: int32 [10, 8], P(None, 'dp'), may hold values from 0 to 999
- w_query: bfloat16 [8, 1536, 1536], P('pipe', ('seq', 'dp')), may hold values from -1 to 1, as said below
- w_keyval: bfloat16 [8, 1536, 1536], P('pipe', ('seq', 'dp')), may hold values from -1 to 1, as said below
- norm_gain: float32 [8, 1536], P('pipe'), may hold values from 0.5 to 1.5
- time_freq: float32 [8, 1536], P('pipe'), may hold values from 0.0005 to 0.05
- contact_table: bfloat16 [8, 16, 1536], P('pipe'), may hold values from -3 to 3
- key_bias: float32 [8, 16], P('pipe'), may hold values from 0.5 to 4
- attn_gate: float32 [8, 1536], P('pipe'), may hold values from 1 to 4
- head_cotangent: bfloat16 [8, 3, 8, 1024, 256], P('pipe', None, 'dp', 'seq'), may hold values from -6 to 6
Outputs:
- section_out: bfloat16 [8, 3, 8, 1024, 1536], P('pipe', None, 'dp', 'seq')
- head_grad: float32 [8, 1536, 256], P('pipe', ('seq', 'dp'))
The draws below stay inside these ranges and needn't reach their ends.
Inputs may be any that keep to these rules, and one draw needn't show every extreme that they name: `contacts`: each frame's contact state, four limbs as bits. `incoming`: activations of order one. `w_query`: entries of about 1536 ** -0.5. `w_keyval`: entries of about 1536 ** -0.5.
All inputs are finite; a program needn't handle non-finite values. No bound on the sum of `keyframes` on one device may be relied on, other than what follows from the above.
Results may differ from the reference program's by a relative error of at most 0.014.
Values may be sent and summed in bfloat16 or wider, within the bound.
A program may use at most 64 MiB of HBM per device.

```python
import math
import jax
import jax.numpy as jnp
from jax import lax

D = 1536
HEADS = 16
HEAD = 96
KVHEADS = 8
F = 256
CONTACTS = 16
TSTEPS = 1000
TURNS = 3
SECTIONS = 8
REPLICAS = 8
FRAMES = 1024
BATCHES = 10


def draw_incoming(key, part):
    own_key = jax.random.fold_in(key, 11)
    normal_key = jax.random.fold_in(own_key, 0)
    shape = (SECTIONS, TURNS, REPLICAS, FRAMES, D)
    values = jax.random.truncated_normal(normal_key, -6.0, 6.0, shape, dtype=jnp.float32)
    return jnp.clip(values, -9.0, 9.0).astype(jnp.bfloat16)


def draw_w_query(key, part):
    own_key = jax.random.fold_in(key, 23)
    values = jax.random.truncated_normal(own_key, -6.0, 6.0, (SECTIONS, D, D), dtype=jnp.float32) * D ** (-0.5)
    return jnp.clip(values, -1.0, 1.0).astype(jnp.bfloat16)


def draw_w_keyval(key, part):
    own_key = jax.random.fold_in(key, 37)
    width = 2 * KVHEADS * HEAD
    values = jax.random.truncated_normal(own_key, -6.0, 6.0, (SECTIONS, D, width), dtype=jnp.float32) * D ** (-0.5)
    return jnp.clip(values, -1.0, 1.0).astype(jnp.bfloat16)


def touch_ends(entries, key, low, largest):
    index_at = [jax.random.randint(jax.random.fold_in(key, axis), (), 0, length) for axis, length in enumerate(entries.shape)]
    widest = entries.shape.index(max(entries.shape))
    next_to = index_at[:widest] + [(index_at[widest] + 1) % entries.shape[widest]] + index_at[widest + 1:]
    return entries.at[tuple(index_at)].set(low).at[tuple(next_to)].set(largest)


def block_levels(key, shape, pieces, low, high):
    def one(position, shards_of):
        heights = jax.random.uniform(jax.random.fold_in(jax.random.fold_in(key, 6), position), (shards_of,), jnp.float32, low / len(pieces), high / len(pieces))
        return jnp.repeat(jnp.exp(heights), shape[position] // shards_of).reshape((-1,) + (1,) * (len(shape) - position - 1))

    loudness = one(*pieces[0])
    for cut in pieces[1:]:
        loudness = loudness * one(*cut)
    return loudness


def normal_values(rng, shape, spread, reach, shards=(), kind=jnp.bfloat16):
    entries = spread * jax.random.normal(rng, shape, jnp.float32)
    if shards:
        entries = entries * block_levels(rng, shape, shards, -0.22, 0.18)
    return jnp.clip(entries, -reach, reach).astype(kind)


def setup_inputs(seed: int = 0) -> dict:
    key_of = jax.random.split(jax.random.key(seed), 13)
    return {
        "incoming": draw_incoming(jax.random.fold_in(key_of[12], 71), 0),
        "contacts": touch_ends(jax.random.randint(key_of[1], (BATCHES, REPLICAS, FRAMES), 0, CONTACTS), jax.random.fold_in(key_of[1], 1), 0, CONTACTS - 1).astype(jnp.int32),
        "keyframes": touch_ends((jax.random.randint(key_of[2], (BATCHES, REPLICAS, FRAMES), 0, 16) < 1).astype(jnp.int32), jax.random.fold_in(key_of[2], 1), 0, 1),
        "timesteps": touch_ends(jax.random.randint(key_of[3], (BATCHES, REPLICAS), 0, TSTEPS), jax.random.fold_in(key_of[3], 1), 0, TSTEPS - 1).astype(jnp.int32),
        "w_query": draw_w_query(jax.random.fold_in(key_of[12], 71), 0),
        "w_keyval": draw_w_keyval(jax.random.fold_in(key_of[12], 71), 0),
        "norm_gain": jnp.clip(1.0 + 0.1 * jax.random.normal(key_of[6], (SECTIONS, D), jnp.float32), 0.5, 1.5),
        "time_freq": jnp.clip(jnp.exp(math.log(0.05) - 4.6051702 * jax.random.uniform(key_of[7], (SECTIONS, D), jnp.float32) ** block_levels(key_of[7], (SECTIONS, D), ((0, 8),), -0.2, 0.2)), 0.0005, 0.05),
        "contact_table": normal_values(key_of[8], (SECTIONS, CONTACTS, D), 0.5, 3.0, ((0, 8),)),
        "key_bias": jnp.clip(0.5 + 3.5 * jax.random.uniform(key_of[9], (SECTIONS, HEADS), jnp.float32) ** block_levels(key_of[9], (SECTIONS, HEADS), ((0, 8),), -0.2, 0.2), 0.5, 4.0),
        "attn_gate": jnp.clip(jnp.exp(math.log(4.0) - 1.3862944 * jax.random.uniform(key_of[10], (SECTIONS, D), jnp.float32) ** block_levels(key_of[10], (SECTIONS, D), ((0, 8),), -0.2, 0.2)), 1.0, 4.0),
        "head_cotangent": normal_values(key_of[11], (SECTIONS, TURNS, REPLICAS, FRAMES, F), 1.0, 6.0, ((0, 8), (2, 8), (3, 8))),
    }


epsilon = 1e-06

def attend(queries, keyval, key_flags, bias_heads):
    queries_f = queries.reshape(FRAMES, HEADS, HEAD).astype(jnp.float32)
    keyval_f = keyval.reshape(FRAMES, KVHEADS, 2, HEAD).astype(jnp.float32)
    group_size = HEADS // KVHEADS
    key_rows = jnp.repeat(keyval_f[:, :, 0], group_size, axis=1)
    value_rows = jnp.repeat(keyval_f[:, :, 1], group_size, axis=1)
    scores = jnp.einsum('qhd,khd->hqk', queries_f, key_rows) * HEAD ** (-0.5)
    scores = scores + bias_heads[:, None, None] * key_flags.astype(jnp.float32)[None, None, :]
    row_max = lax.optimization_barrier(jnp.max(scores, axis=-1, keepdims=True))
    exponent = jnp.exp(scores - row_max)
    probabilities = (exponent / lax.optimization_barrier(jnp.sum(exponent, axis=-1, keepdims=True))).astype(jnp.bfloat16)
    attended = jnp.einsum('hqk,khd->qhd', probabilities.astype(jnp.float32), value_rows)
    return attended.astype(jnp.bfloat16).reshape(FRAMES, D)

def section_apply(current, contact_rows, key_flags, timestep, wquery, wkeyval, gain_row, freq_row, table, bias_heads, gate_row):
    onehot = (contact_rows[..., None] == jnp.arange(CONTACTS)[None, None, :]).astype(jnp.float32)
    embedded = jnp.einsum('rfc,cd->rfd', onehot, table.astype(jnp.float32))
    hidden = current.astype(jnp.float32) + embedded
    root_mean = jnp.sqrt(lax.optimization_barrier(jnp.mean(hidden * hidden, axis=-1, keepdims=True)) + epsilon)
    modulation = gain_row[None, :] * (1.0 + 0.5 * jnp.sin(timestep.astype(jnp.float32)[:, None] * freq_row[None, :]))
    normed = (hidden / root_mean * modulation[:, None, :]).astype(jnp.bfloat16)
    flat = normed.reshape(REPLICAS * FRAMES, D)
    queries = jnp.dot(flat, wquery, preferred_element_type=jnp.float32).astype(jnp.bfloat16)
    keyval = jnp.dot(flat, wkeyval, preferred_element_type=jnp.float32).astype(jnp.bfloat16)
    queries = queries.reshape(REPLICAS, FRAMES, D)
    keyval = keyval.reshape(REPLICAS, FRAMES, 2 * KVHEADS * HEAD)
    attended = lax.map(lambda items: attend(items[0], items[1], items[2], bias_heads), (queries, keyval, key_flags))
    return (hidden + gate_row[None, None, :] * attended.astype(jnp.float32)).astype(jnp.bfloat16)

def reference(incoming, contacts, keyframes, timesteps, w_query, w_keyval, norm_gain, time_freq, contact_table, key_bias, attn_gate, head_cotangent):
    factor = float(TURNS * REPLICAS * FRAMES) ** (-0.5)
    results = []
    grads = []
    previous = None
    for section_idx in range(SECTIONS):
        current_row = []
        for turn in range(TURNS):
            if section_idx == 0 or turn == 0:
                current = incoming[section_idx, turn]
            else:
                current = previous[turn - 1]
            batch_idx = turn - section_idx + SECTIONS - 1
            output = section_apply(current, contacts[batch_idx], keyframes[batch_idx], timesteps[batch_idx], w_query[section_idx], w_keyval[section_idx], norm_gain[section_idx], time_freq[section_idx], contact_table[section_idx], key_bias[section_idx], attn_gate[section_idx])
            current_row.append(output)
        stacked = jnp.stack(current_row)
        results.append(stacked)
        grad = jnp.dot(stacked.reshape(TURNS * REPLICAS * FRAMES, D).T, head_cotangent[section_idx].reshape(TURNS * REPLICAS * FRAMES, F), preferred_element_type=jnp.float32) * factor
        grads.append(grad)
        previous = current_row
    return (jnp.stack(results), jnp.stack(grads))
```

```python
import functools
import math

import jax
import jax.numpy as jnp
from jax import lax
from jax.experimental import pallas as pl
from jax.experimental.pallas import tpu as pltpu
from jax.sharding import PartitionSpec as P

BF16 = jnp.bfloat16
F32 = jnp.float32
MESH = pl.DeviceIdType.MESH
EPSILON = 1e-06
LOG2E = math.log2(math.e)
XN = 4
ZN = 8
SN = 8
TURNS = 3
D = 1536
CW = 384
HEAD = 96
B = 128


def dot(a, b):
    return jnp.dot(a, b, preferred_element_type=F32)


def dot_t(a, b):
    return lax.dot_general(a, b, (((0,), (0,)), ((), ())), preferred_element_type=F32)


def dot_nt(a, b):
    return lax.dot_general(a, b, (((1,), (1,)), ((), ())), preferred_element_type=F32)


def kernel(
    inc, contacts, keyframes, timesteps, wq, wkv, gain, freq, table, kbias, gate, cot,
    out, grad,
    xg, wr, wp, ctv, cotv, stg, rcv, act, asend, arecv, atto, ob, modv, psel, pw, qpad, gacc, grec, gsum, grz,
    xs, xrv, lx, ys, yr, ws, wrv, wl, zs, zr, bs, br, cs, cr, ks, kr, qs, qr, asm, arm, osm, orm, gs, gr,
):
    s = lax.axis_index("pipe")
    i = lax.axis_index("seq")
    j = lax.axis_index("dp")
    x = lax.div(i, 2)
    c = lax.rem(i, 2)
    first = lax.div(SN - s, SN)

    def xat(d):
        return lax.rem(x + d + XN, XN)

    def zat(d):
        return lax.rem(j + d + ZN, ZN)

    def xdev(d):
        return (s, 2 * xat(d) + c, j)

    def zdev(d):
        return (s, i, zat(d))

    sib = (s, 2 * x + 1 - c, j)
    ynext = (lax.rem(s + 1, SN), i, j)
    yprev = (lax.rem(s + SN - 1, SN), i, j)

    def remote(src, dst, send, recv, device):
        return pltpu.make_async_remote_copy(
            src_ref=src, dst_ref=dst, send_sem=send, recv_sem=recv, device_id=device, device_id_type=MESH
        )

    def cols(b):
        return pl.ds(pl.multiple_of(b * CW, 128), CW)

    def rows(r):
        return pl.ds(pl.multiple_of(r * B, B), B)

    barrier = pltpu.get_barrier_semaphore()
    peers = [xdev(1), xdev(2), xdev(3), sib, ynext, yprev] + [zdev(d) for d in range(1, ZN)]
    for peer in peers:
        pl.semaphore_signal(barrier, inc=1, device_id=peer, device_id_type=MESH)

    own_x0 = pltpu.make_async_copy(inc.at[0, 0, 0], xg.at[0, rows(x)], lx.at[0])
    own_x0.start()
    own_ct = pltpu.make_async_copy(contacts, ctv.at[x], cs.at[0])
    own_ct.start()
    own_cot = pltpu.make_async_copy(cot.at[0, :, 0], cotv.at[x], lx.at[3])
    own_cot.start()
    own_w = [
        pltpu.make_async_copy(w.at[0, :, cols(x)], wr.at[c, j, x, :, CW * n : CW * n + CW], wl.at[n])
        for n, w in enumerate((wq, wkv))
    ]
    for copy in own_w:
        copy.start()

    def own_later(t):
        return pltpu.make_async_copy(inc.at[0, t, 0], xg.at[t, rows(x)], lx.at[t])

    @pl.when(s == 0)
    def _():
        own_later(1).start()
        own_later(2).start()

    pl.semaphore_wait(barrier, len(peers))

    def w_piece(d, n, w):
        return remote(
            w.at[0, :, cols(xat(d))],
            wr.at[c, j, x, :, CW * n : CW * n + CW],
            ws.at[d - 1, n],
            wrv.at[d - 1, n],
            xdev(d),
        )

    def w_arrival(d, n):
        here = wr.at[c, j, xat(-d), :, CW * n : CW * n + CW]
        return remote(here, here, ws.at[d - 1, n], wrv.at[d - 1, n], xdev(d))

    for d in (1, 3, 2):
        for n, w in enumerate((wq, wkv)):
            w_piece(d, n, w).start()

    def ct_piece(d, src):
        return remote(ctv.at[src], ctv.at[src], cs.at[d], cr.at[d], xdev(d))

    def cot_piece(t, d, src):
        return remote(cotv.at[src, t], cotv.at[src, t], ks.at[t, d - 1], kr.at[t, d - 1], xdev(d))

    def piece(t, a, b):
        if t == 0:
            r, n = b, a
        else:
            r, n = a + first * (b - a), b + first * (a - b)
        return xg.at[t, rows(r), cols(n)]

    def x_send(t, a, way):
        dst = piece(t, a, x)
        src = inc.at[0, 0, 0, :, CW * a : CW * a + CW] if t == 0 else dst
        return remote(src, dst, xs.at[t, a, way], xrv.at[t, a, way], xdev(1 - 2 * way))

    def x_arrival(t, a, way):
        here = piece(t, a, xat(2 * way - 1))
        return remote(here, here, xs.at[t, a, way], xrv.at[t, a, way], xdev(1))

    def x_pass(t, a):
        way = a % 2
        here = piece(t, a, xat(2 * way - 1))
        return remote(here, here, xs.at[t, a, 2], xrv.at[t, a, 2], xdev(1 - 2 * way))

    def x_passed(t, a):
        here = piece(t, a, xat(2))
        return remote(here, here, xs.at[t, a, 2], xrv.at[t, a, 2], xdev(1))

    def y_copy(t, r):
        return remote(ob.at[t, r], xg.at[t + 1, rows(r), cols(x)], ys.at[t, r], yr.at[t, r], ynext)

    def x_start(t, a):
        if t > 0:
            @pl.when(s > 0)
            def _():
                y_copy(t - 1, a).wait_recv()

            if a == 0:
                @pl.when(s == 0)
                def _():
                    own_later(t).wait()

        x_send(t, a, 0).start()
        x_send(t, a, 1).start()

    def x_forward(t, a):
        x_arrival(t, a, a % 2).wait_recv()
        x_pass(t, a).start()

    def x_finish(t, a):
        x_arrival(t, a, 1 - a % 2).wait_recv()
        x_passed(t, a).wait_recv()

    for a in range(XN):
        x_start(0, a)
    own_ct.wait()
    for d in (1, 2, 3):
        ct_piece(d, x).start()

    lane = lax.broadcasted_iota(jnp.int32, (1, 128), 1)
    head_lane = lax.broadcasted_iota(jnp.int32, (1, 16), 1)
    for h in range(4):
        b = jnp.sum(jnp.where(head_lane == 4 * x + h, kbias[...], 0.0), axis=1, keepdims=True) * LOG2E
        high = b.astype(BF16).astype(F32)
        qpad[h : h + 1, :] = jnp.where(lane == HEAD, high, 0.0) + jnp.where(lane == HEAD + 1, b - high, 0.0)
    for t in range(TURNS):
        step = timesteps[t - s + SN - 1, 0].astype(F32)
        modv[t : t + 1, :] = gain[...] * (1.0 + 0.5 * jnp.sin(step * freq[...]))
    row = lax.broadcasted_iota(jnp.int32, (512, CW), 0)
    col = lax.broadcasted_iota(jnp.int32, (512, CW), 1)
    slot = lax.shift_right_logical(row, 7)
    low = row - slot * 128
    head = jnp.where(slot < 2, slot + 2 * c, slot - 2 * c)
    psel[...] = jnp.where((low < HEAD) & (col == head * HEAD + low), 1.0, 0.0).astype(BF16)
    row = lax.broadcasted_iota(jnp.int32, (CW, 512), 0)
    col = lax.broadcasted_iota(jnp.int32, (CW, 512), 1)
    slot = lax.shift_right_logical(col, 7)
    low = col - slot * 128
    pw[...] = jnp.where((low < HEAD) & (row == slot * HEAD + low), 1.0, 0.0).astype(BF16)

    def z_blocks(k, way):
        block = zat(-k) if way == 0 else zat(k)
        part = wr.at[c, block] if k < ZN // 2 else wr.at[c, block, pl.ds(2 * way, 2)]
        return part

    def z_send(k, way):
        block = zat(1 - k) if way == 0 else zat(k - 1)
        part = wr.at[c, block] if k < ZN // 2 else wr.at[c, block, pl.ds(2 * way, 2)]
        return remote(part, part, zs.at[k - 1, way], zr.at[k - 1, way], zdev(1 - 2 * way))

    def z_arrival(k, way):
        part = z_blocks(k, way)
        return remote(part, part, zs.at[k - 1, way], zr.at[k - 1, way], zdev(1))

    def sib_part(core, k, way):
        block = zat(-k) if way == 0 else zat(k)
        return wr.at[core, block] if k < ZN // 2 else wr.at[core, block, pl.ds(2 * way, 2)]

    def sib_send(core, k, way):
        part = sib_part(core, k, way)
        return remote(part, part, bs.at[k, way], br.at[k, way], sib)

    for copy in own_w:
        copy.wait()
    for d in (1, 3, 2):
        for n in range(2):
            w_arrival(d, n).wait_recv()
    z_send(1, 0).start()
    z_send(1, 1).start()
    sib_send(c, 0, 0).start()
    x_forward(0, 0)
    x_forward(0, 1)

    def z_step(k):
        for way in range(2):
            z_arrival(k, way).wait_recv()
            if k < ZN // 2:
                z_send(k + 1, way).start()
            sib_send(c, k, way).start()

    z_step(1)
    x_forward(0, 2)
    x_forward(0, 3)
    for k in range(2, ZN // 2 + 1):
        z_step(k)
    own_x0.wait()
    for a in range(XN):
        x_finish(0, a)
    for d in (1, 2, 3):
        ct_piece(d, xat(-d)).wait_recv()
    sib_send(1 - c, 0, 0).wait_recv()
    for k in range(1, ZN // 2 + 1):
        for way in range(2):
            sib_send(1 - c, k, way).wait_recv()

    def prepare(n, _):
        cc, xx = lax.rem(n, 2), lax.div(n, 2)
        block = wr[cc, :, xx].astype(F32).reshape(ZN * 24, 2 * CW).astype(BF16)
        dst = pl.ds(pl.multiple_of(n * 192, 64), 192)
        wp[dst, 0:512] = dot(block[:, :CW], pw[...]).astype(BF16)
        wp[dst, 512:1024] = dot(block[:, CW:], pw[...]).astype(BF16)
        return 0

    lax.fori_loop(0, 2 * XN, prepare, 0)

    def contact_rows(t, r):
        return ctv[r, t - s + SN - 1]

    def onehot(values):
        count = values.shape[1]
        states = lax.broadcasted_iota(jnp.int32, (16, count), 0)
        return jnp.where(states == values, 1.0, 0.0).astype(BF16)

    place = lax.broadcasted_iota(jnp.int32, (16, 128), 0)
    place_lane = lax.broadcasted_iota(jnp.int32, (16, 128), 1)
    flag_lanes = jnp.where(
        (place == 0) & ((place_lane == HEAD) | (place_lane == HEAD + 1)), 1.0, 0.0
    ).astype(BF16)
    ones_lane = jnp.where(lane == HEAD, 1.0, 0.0)

    def q_exchange(t, p):
        span = pl.ds(256 * p, 256)
        return remote(stg.at[t, 1 - c, :, span], rcv.at[t, :, span], qs.at[t, p], qr.at[t, p], sib)

    def project(t, p):
        turn = t - s + SN - 1
        span = slice(256 * p, 256 * p + 256)
        flags = []
        scales = []
        for q in range(2):
            r = 2 * p + q
            inner = slice(B * r, B * r + B)
            hidden = xg[t, inner, :].astype(F32) + dot_t(onehot(contact_rows(t, r)), table[0])
            square = jnp.sum(hidden * hidden, axis=1, keepdims=True)
            act[inner, :] = (hidden * modv[t : t + 1, :]).astype(BF16)
            scales.append(lax.rsqrt(square * (1.0 / D) + EPSILON))
            flag = keyframes[turn, :, pl.ds(pl.multiple_of((2 * r + c) * B, B), B)]
            flag = jnp.where(place == 0, flag.astype(F32), 0.0).astype(BF16)
            flags.append(dot_t(flag, flag_lanes))
        scale = jnp.concatenate(scales, axis=0)
        flag = jnp.concatenate(flags, axis=0)
        result = dot(act[span, :], wp[...])
        scale_q = scale * (LOG2E * HEAD ** (-0.5))
        for h in range(4):
            stg[t, h // 2, h % 2, span, :] = (
                result[:, 128 * h : 128 * h + 128] * scale_q + qpad[h : h + 1, :]
            ).astype(BF16)
        for h in range(2):
            at = 512 + 256 * h
            stg[t, h, 2, span, :] = (result[:, at : at + 128] * scale + flag).astype(BF16)
            stg[t, h, 3, span, :] = (result[:, at + 128 : at + 256] * scale + ones_lane).astype(BF16)
        q_exchange(t, p).start()

    def a_exchange(t, r):
        return remote(asend.at[t, r], arecv.at[t, r], asm.at[t, r], arm.at[t, r], sib)

    def attend(t, r):
        for h in range(2):
            q = jnp.concatenate([stg[t, c, h, rows(r), :], rcv[t, h, rows(r), :]], axis=0)
            s0 = dot_nt(q, stg[t, c, 2])
            s1 = dot_nt(q, rcv[t, 2])
            top = jnp.maximum(jnp.max(s0, axis=1, keepdims=True), jnp.max(s1, axis=1, keepdims=True))
            total = dot(jnp.exp2(s0 - top).astype(BF16), stg[t, c, 3])
            total = total + dot(jnp.exp2(s1 - top).astype(BF16), rcv[t, 3])
            result = (total * (1.0 / total[:, HEAD : HEAD + 1])).astype(BF16)
            atto[r, h] = result[:B]
            asend[t, r, h] = result[B:]
        a_exchange(t, r).start()

    def finish(t, r):
        a_exchange(t, r).wait_recv()
        heads = jnp.concatenate([atto[r, 0], atto[r, 1], arecv[t, r, 0], arecv[t, r, 1]], axis=1)
        attended = dot(heads, psel[...])
        hidden = xg[t, rows(r), cols(x)].astype(F32) + dot_t(
            onehot(contact_rows(t, r)), table[0, :, cols(x)]
        )
        ob[t, r] = (hidden + gate[:, cols(x)] * attended).astype(BF16)
        if t + 1 < TURNS:
            @pl.when(s < SN - 1)
            def _():
                y_copy(t, r).start()

    def out_copy(t, d):
        return remote(
            ob.at[t, xat(d)], out.at[0, t, 0, :, cols(x)], osm.at[t, d], orm.at[t, d], xdev(d)
        )

    def out_arrival(t, d):
        return remote(
            ob.at[t, xat(d)], out.at[0, t, 0, :, cols(xat(-d))], osm.at[t, d], orm.at[t, d], xdev(d)
        )

    def out_own(t):
        return pltpu.make_async_copy(ob.at[t, x], out.at[0, t, 0, :, cols(x)], osm.at[t, 0])

    for t in range(TURNS):
        if t > 0:
            x_forward(t, 0)
            x_forward(t, 1)
            x_start(t, 2)
            x_start(t, 3)
            x_forward(t, 2)
            x_forward(t, 3)
            for a in range(XN):
                x_finish(t, a)
        project(t, 0)
        project(t, 1)
        if t == 0:
            own_cot.wait()
        for d in (1, 2, 3):
            cot_piece(t, d, x).start()
        if t > 0:
            out_own(t - 1).start()
            for d in (1, 2, 3):
                out_copy(t - 1, d).start()
        q_exchange(t, 0).wait_recv()
        q_exchange(t, 1).wait_recv()

        def step(r, _, t=t):
            attend(t, r)

            @pl.when(r > 0)
            def _():
                finish(t, r - 1)

            return 0

        lax.fori_loop(0, XN, step, 0)
        if t + 1 < TURNS:
            x_start(t + 1, 0)
        finish(t, XN - 1)
        if t + 1 < TURNS:
            x_start(t + 1, 1)
        else:
            out_own(t).start()
            for d in (1, 2, 3):
                out_copy(t, d).start()
        for d in (1, 2, 3):
            cot_piece(t, d, xat(-d)).wait_recv()
        share = dot_t(ob[t].reshape(XN * B, CW), cotv[:, t].reshape(XN * B, 256))
        gacc[...] = share if t == 0 else gacc[...] + share

    g_sib = remote(
        gacc.at[pl.ds(pl.multiple_of((1 - c) * 192, 64), 192)], grec, gs.at[0], gr.at[0], sib
    )
    g_sib.start()
    g_sib.wait_recv()
    gsum[...] = gacc[pl.ds(pl.multiple_of(c * 192, 64), 192), :] + grec[...]

    def g_copy(d):
        return remote(
            gsum.at[pl.ds(pl.multiple_of(24 * zat(d), 8), 24)], grz.at[d - 1], gs.at[d], gr.at[d], zdev(d)
        )

    for d in (4, 3, 5, 2, 6, 1, 7):
        g_copy(d).start()
    total = gsum[pl.ds(pl.multiple_of(24 * j, 8), 24), :]
    for d in (1, 7, 2, 6, 3, 5, 4):
        g_copy(d).wait_recv()
        total = total + grz[d - 1]
    grad[0] = total * (float(TURNS * ZN * 1024) ** (-0.5))

    for d in (1, 2, 3):
        for n, w in enumerate((wq, wkv)):
            w_piece(d, n, w).wait_send()
        ct_piece(d, x).wait_send()
    for k in range(ZN // 2 + 1):
        for way in range(2):
            if k > 0:
                z_send(k, way).wait_send()
            if k > 0 or way == 0:
                sib_send(c, k, way).wait_send()
    for t in range(TURNS):
        out_own(t).wait()
        for d in (1, 2, 3):
            cot_piece(t, d, x).wait_send()
            out_copy(t, d).wait_send()
            out_arrival(t, d).wait_recv()
        for a in range(XN):
            x_send(t, a, 0).wait_send()
            x_send(t, a, 1).wait_send()
            x_pass(t, a).wait_send()
            a_exchange(t, a).wait_send()
        q_exchange(t, 0).wait_send()
        q_exchange(t, 1).wait_send()
    @pl.when(s < SN - 1)
    def _():
        for t in range(TURNS - 1):
            for a in range(XN):
                y_copy(t, a).wait_send()

    g_sib.wait_send()
    for d in range(1, ZN):
        g_copy(d).wait_send()


def body(*args):
    vmem = pl.BlockSpec(memory_space=pltpu.VMEM)
    smem = pl.BlockSpec(memory_space=pltpu.SMEM)
    anys = pl.BlockSpec(memory_space=pl.ANY)
    dma = pltpu.SemaphoreType.DMA
    return pl.pallas_call(
        kernel,
        out_shape=(
            jax.ShapeDtypeStruct((1, TURNS, 1, B, D), BF16),
            jax.ShapeDtypeStruct((1, 24, 256), F32),
        ),
        in_specs=[anys, anys, vmem, smem, anys, anys, vmem, vmem, vmem, vmem, vmem, anys],
        out_specs=(anys, vmem),
        scratch_shapes=[
            pltpu.VMEM((TURNS, 4 * B, D), BF16),
            pltpu.VMEM((2, ZN, XN, 24, 2 * CW), BF16),
            pltpu.VMEM((D, 1024), BF16),
            pltpu.VMEM((XN, 10, 1, B), jnp.int32),
            pltpu.VMEM((XN, TURNS, B, 256), BF16),
            pltpu.VMEM((TURNS, 2, 4, 4 * B, 128), BF16),
            pltpu.VMEM((TURNS, 4, 4 * B, 128), BF16),
            pltpu.VMEM((4 * B, D), BF16),
            pltpu.VMEM((TURNS, XN, 2, B, 128), BF16),
            pltpu.VMEM((TURNS, XN, 2, B, 128), BF16),
            pltpu.VMEM((XN, 2, B, 128), BF16),
            pltpu.VMEM((TURNS, XN, B, CW), BF16),
            pltpu.VMEM((8, D), F32),
            pltpu.VMEM((512, CW), BF16),
            pltpu.VMEM((CW, 512), BF16),
            pltpu.VMEM((8, 128), F32),
            pltpu.VMEM((CW, 256), F32),
            pltpu.VMEM((192, 256), F32),
            pltpu.VMEM((192, 256), F32),
            pltpu.VMEM((ZN - 1, 24, 256), F32),
            dma((TURNS, XN, 3)),
            dma((TURNS, XN, 3)),
            dma((4,)),
            dma((TURNS - 1, XN)),
            dma((TURNS - 1, XN)),
            dma((3, 2)),
            dma((3, 2)),
            dma((2,)),
            dma((4, 2)),
            dma((4, 2)),
            dma((5, 2)),
            dma((5, 2)),
            dma((4,)),
            dma((4,)),
            dma((TURNS, 3)),
            dma((TURNS, 3)),
            dma((TURNS, 2)),
            dma((TURNS, 2)),
            dma((TURNS, XN)),
            dma((TURNS, XN)),
            dma((TURNS, XN)),
            dma((TURNS, XN)),
            dma((ZN,)),
            dma((ZN,)),
        ],
        compiler_params=pltpu.CompilerParams(
            collective_id=0, has_side_effects=True, vmem_limit_bytes=56 * 1024 * 1024
        ),
        cost_estimate=pl.CostEstimate(
            flops=10_000_000_000, bytes_accessed=16_000_000, transcendentals=7_000_000
        ),
    )(*args)


def solution(mesh):
    in_specs = (
        P("pipe", None, "dp", "seq", None),
        P(None, "dp", "seq"),
        P(None, "dp", None),
        P(None, "dp"),
        P("pipe", ("seq", "dp"), None),
        P("pipe", ("seq", "dp"), None),
        P("pipe", None),
        P("pipe", None),
        P("pipe", None, None),
        P("pipe", None),
        P("pipe", None),
        P("pipe", None, "dp", "seq", None),
    )
    out_specs = (P("pipe", None, "dp", "seq", None), P("pipe", ("seq", "dp"), None))
    return jax.shard_map(body, mesh=mesh, in_specs=in_specs, out_specs=out_specs, check_vma=False)
```

```python
import functools
import math

import jax
import jax.numpy as jnp
from jax import lax
from jax.experimental import pallas as pl
from jax.experimental.pallas import tpu as pltpu
from jax.sharding import PartitionSpec as P

BF16 = jnp.bfloat16
F32 = jnp.float32
MESH = pl.DeviceIdType.MESH
EPSILON = 1e-06
LOG2E = math.log2(math.e)
XN = 4
ZN = 8
SN = 8
TURNS = 3
ORDER = (0, 1, 3, 2)
SKEW = 3
FORWARD_AT = (4, 7, 10, 13)
D = 1536
CW = 384
HEAD = 96
B = 128


def dot(a, b):
    return jnp.dot(a, b, preferred_element_type=F32)


def dot_t(a, b):
    return lax.dot_general(a, b, (((0,), (0,)), ((), ())), preferred_element_type=F32)


def dot_nt(a, b):
    return lax.dot_general(a, b, (((1,), (1,)), ((), ())), preferred_element_type=F32)


def kernel(
    inc, contacts, keyframes, timesteps, wq, wkv, gain, freq, table, kbias, gate, cot,
    out, grad,
    xg, wr, wp, ctv, cotv, stg, rcv, act, scales, asend, arecv, atto, ob, modv, psel, pw, qpad, gacc, grec, gsum, gpass, grz,
    xs, xrv, lx, ys, yr, ws, wrv, wl, zs, zr, bs, br, cs, cr, ks, kr, qs, qr, asm, arm, osm, orm, gs, gr,
):
    s = lax.axis_index("pipe")
    i = lax.axis_index("seq")
    j = lax.axis_index("dp")
    x = lax.div(i, 2)
    c = lax.rem(i, 2)
    first = lax.div(SN - s, SN)

    def xat(d):
        return lax.rem(x + d + XN, XN)

    def zat(d):
        return lax.rem(j + d + ZN, ZN)

    def xdev(d):
        return (s, 2 * xat(d) + c, j)

    def zdev(d):
        return (s, i, zat(d))

    sib = (s, 2 * x + 1 - c, j)
    ynext = (lax.rem(s + 1, SN), i, j)
    yprev = (lax.rem(s + SN - 1, SN), i, j)

    def remote(src, dst, send, recv, device):
        return pltpu.make_async_remote_copy(
            src_ref=src, dst_ref=dst, send_sem=send, recv_sem=recv, device_id=device, device_id_type=MESH
        )

    def cols(b):
        return pl.ds(pl.multiple_of(b * CW, 128), CW)

    def rows(r):
        return pl.ds(pl.multiple_of(r * B, B), B)

    barrier = pltpu.get_barrier_semaphore()
    peers = [xdev(1), xdev(2), xdev(3), sib, ynext, yprev] + [zdev(d) for d in range(1, ZN)]
    for peer in peers:
        pl.semaphore_signal(barrier, inc=1, device_id=peer, device_id_type=MESH)

    own_x0 = pltpu.make_async_copy(inc.at[0, 0, 0], xg.at[0, rows(x)], lx.at[0])
    own_x0.start()
    own_ct = pltpu.make_async_copy(contacts, ctv.at[x], cs.at[0])
    own_ct.start()
    own_cot = pltpu.make_async_copy(cot.at[0, :, 0], cotv.at[x], lx.at[3])
    own_cot.start()
    own_w = [
        pltpu.make_async_copy(w.at[0, :, cols(x)], wr.at[c, j, x, :, CW * n : CW * n + CW], wl.at[n])
        for n, w in enumerate((wq, wkv))
    ]
    for copy in own_w:
        copy.start()

    def own_later(t):
        return pltpu.make_async_copy(inc.at[0, t, 0], xg.at[t, rows(x)], lx.at[t])

    @pl.when(s == 0)
    def _():
        own_later(1).start()
        own_later(2).start()

    pl.semaphore_wait(barrier, len(peers))

    def w_piece(d, n, w):
        return remote(
            w.at[0, :, cols(xat(d))],
            wr.at[c, j, x, :, CW * n : CW * n + CW],
            ws.at[d - 1, n],
            wrv.at[d - 1, n],
            xdev(d),
        )

    def w_arrival(d, n):
        here = wr.at[c, j, xat(-d), :, CW * n : CW * n + CW]
        return remote(here, here, ws.at[d - 1, n], wrv.at[d - 1, n], xdev(d))

    for d in (1, 3, 2):
        for n, w in enumerate((wq, wkv)):
            w_piece(d, n, w).start()

    def ct_piece(d, src):
        return remote(ctv.at[src], ctv.at[src], cs.at[d], cr.at[d], xdev(d))

    def cot_piece(t, d, src):
        return remote(cotv.at[src, t], cotv.at[src, t], ks.at[t, d - 1], kr.at[t, d - 1], xdev(d))

    def piece(t, a, b):
        if t == 0:
            r, n = b, a
        else:
            r, n = a + first * (b - a), b + first * (a - b)
        return xg.at[t, rows(r), cols(n)]

    def x_send(t, a, way):
        dst = piece(t, a, x)
        src = inc.at[0, 0, 0, :, CW * a : CW * a + CW] if t == 0 else dst
        return remote(src, dst, xs.at[t, a, way], xrv.at[t, a, way], xdev(1 - 2 * way))

    def x_arrival(t, a, way):
        here = piece(t, a, xat(2 * way - 1))
        return remote(here, here, xs.at[t, a, way], xrv.at[t, a, way], xdev(1))

    def x_pass(t, a):
        way = a % 2
        here = piece(t, a, xat(2 * way - 1))
        return remote(here, here, xs.at[t, a, 2], xrv.at[t, a, 2], xdev(1 - 2 * way))

    def x_passed(t, a):
        here = piece(t, a, xat(2))
        return remote(here, here, xs.at[t, a, 2], xrv.at[t, a, 2], xdev(1))

    def y_copy(t, r):
        return remote(ob.at[t, r], xg.at[t + 1, rows(r), cols(x)], ys.at[t, r], yr.at[t, r], ynext)

    def x_start(t, a):
        if t > 0:
            @pl.when(s > 0)
            def _():
                y_copy(t - 1, a).wait_recv()

            if a == 0:
                @pl.when(s == 0)
                def _():
                    own_later(t).wait()

        x_send(t, a, 0).start()
        x_send(t, a, 1).start()

    def x_forward(t, a):
        x_arrival(t, a, a % 2).wait_recv()
        x_pass(t, a).start()

    def x_finish(t, a):
        x_arrival(t, a, 1 - a % 2).wait_recv()
        x_passed(t, a).wait_recv()

    for a in range(XN):
        x_start(0, a)
    own_ct.wait()
    for d in (1, 2, 3):
        ct_piece(d, x).start()

    lane = lax.broadcasted_iota(jnp.int32, (1, 128), 1)
    head_lane = lax.broadcasted_iota(jnp.int32, (1, 16), 1)
    for h in range(4):
        b = jnp.sum(jnp.where(head_lane == 4 * x + h, kbias[...], 0.0), axis=1, keepdims=True) * LOG2E
        high = b.astype(BF16).astype(F32)
        qpad[h : h + 1, :] = jnp.where(lane == HEAD, high, 0.0) + jnp.where(lane == HEAD + 1, b - high, 0.0)
    for t in range(TURNS):
        step = timesteps[0, t - s + SN - 1].astype(F32)
        modv[t : t + 1, :] = gain[...] * (1.0 + 0.5 * jnp.sin(step * freq[...]))
    row = lax.broadcasted_iota(jnp.int32, (512, CW), 0)
    col = lax.broadcasted_iota(jnp.int32, (512, CW), 1)
    slot = lax.shift_right_logical(row, 7)
    low = row - slot * 128
    head = jnp.where(slot < 2, slot + 2 * c, slot - 2 * c)
    psel[...] = jnp.where((low < HEAD) & (col == head * HEAD + low), 1.0, 0.0).astype(BF16)
    row = lax.broadcasted_iota(jnp.int32, (CW, 512), 0)
    col = lax.broadcasted_iota(jnp.int32, (CW, 512), 1)
    slot = lax.shift_right_logical(col, 7)
    low = col - slot * 128
    pw[...] = jnp.where((low < HEAD) & (row == slot * HEAD + low), 1.0, 0.0).astype(BF16)

    half = ZN // 2

    def part(core, xx, zz, k, way):
        block = wr.at[core, zz, xx]
        return block if k < half else block.at[:, pl.ds(CW * way, CW)]

    def came(k, way):
        return zat(-k) if way == 0 else zat(k)

    def z_send(n, k, way):
        ref = part(c, xat(ORDER[n]), zat(1 - k) if way == 0 else zat(k - 1), k, way)
        return remote(ref, ref, zs.at[n, k - 1, way], zr.at[n, k - 1, way], zdev(1 - 2 * way))

    def z_arrival(n, k, way):
        ref = part(c, xat(ORDER[n]), came(k, way), k, way)
        return remote(ref, ref, zs.at[n, k - 1, way], zr.at[n, k - 1, way], zdev(1))

    def sib_send(core, n, k, way):
        ref = part(core, xat(ORDER[n]), came(k, way), k, way)
        return remote(ref, ref, bs.at[n, k, way], br.at[n, k, way], sib)

    def z_step(n, k):
        if k == 0:
            if n == 0:
                for copy in own_w:
                    copy.wait()
            else:
                w_arrival((XN - ORDER[n]) % XN, 0).wait_recv()
                w_arrival((XN - ORDER[n]) % XN, 1).wait_recv()
            z_send(n, 1, 0).start()
            z_send(n, 1, 1).start()
            sib_send(c, n, 0, 0).start()
            return
        for way in range(2):
            z_arrival(n, k, way).wait_recv()
            if k < half:
                z_send(n, k + 1, way).start()
            sib_send(c, n, k, way).start()

    def prepare(n):
        sib_send(1 - c, n, 0, 0).wait_recv()
        for k in range(1, half + 1):
            for way in range(2):
                sib_send(1 - c, n, k, way).wait_recv()
        xx = xat(ORDER[n])

        def one(cc, _):
            block = wr[cc, :, xx].astype(F32).reshape(ZN * 24, 2 * CW).astype(BF16)
            dst = pl.ds(pl.multiple_of((2 * xx + cc) * 192, 64), 192)
            wp[dst, 0:512] = dot(block[:, :CW], pw[...]).astype(BF16)
            wp[dst, 512:1024] = dot(block[:, CW:], pw[...]).astype(BF16)
            return 0

        lax.fori_loop(0, 2, one, 0)

    steps = sorted((SKEW * k + n, n, k) for n in range(XN) for k in range(half + 1))
    ready = []
    for at, (_, n, k) in enumerate(steps):
        z_step(n, k)
        if at in FORWARD_AT:
            x_forward(0, FORWARD_AT.index(at))
        if ready:
            prepare(ready.pop())
        if k == half:
            ready.append(n)
    own_x0.wait()
    own_cot.wait()
    for a in range(XN):
        x_finish(0, a)
    for t in range(TURNS):
        for d in (1, 2, 3):
            cot_piece(t, d, x).start()
    for d in (1, 2, 3):
        ct_piece(d, xat(-d)).wait_recv()

    def contact_rows(t, r):
        return ctv[r, t - s + SN - 1]

    def onehot(values):
        count = values.shape[1]
        states = lax.broadcasted_iota(jnp.int32, (16, count), 0)
        return jnp.where(states == values, 1.0, 0.0).astype(BF16)

    place = lax.broadcasted_iota(jnp.int32, (16, 128), 0)
    place_lane = lax.broadcasted_iota(jnp.int32, (16, 128), 1)
    flag_lanes = jnp.where(
        (place == 0) & ((place_lane == HEAD) | (place_lane == HEAD + 1)), 1.0, 0.0
    ).astype(BF16)
    ones_lane = jnp.where(lane == HEAD, 1.0, 0.0)

    def q_exchange(t, r):
        span = pl.ds(B * r, B)
        return remote(stg.at[t, 1 - c, :, span], rcv.at[t, :, span], qs.at[t, r], qr.at[t, r], sib)

    def norm(t, r):
        span = slice(B * r, B * r + B)
        hidden = xg[t, span, :].astype(F32) + dot_t(onehot(contact_rows(t, r)), table[0])
        square = jnp.sum(hidden * hidden, axis=1, keepdims=True)
        act[span, :] = (hidden * modv[t : t + 1, :]).astype(BF16)
        scales[span, :] = jnp.broadcast_to(lax.rsqrt(square * (1.0 / D) + EPSILON), (B, 128))

    def project(t, r):
        span = slice(B * r, B * r + B)
        scale = scales[span, :]
        flag = keyframes[t - s + SN - 1, :, pl.ds(pl.multiple_of((2 * r + c) * B, B), B)]
        flag = dot_t(jnp.where(place == 0, flag.astype(F32), 0.0).astype(BF16), flag_lanes)
        result = dot(act[span, :], wp[...])
        scale_q = scale * (LOG2E * HEAD ** (-0.5))
        for h in range(4):
            stg[t, h // 2, h % 2, span, :] = (
                result[:, 128 * h : 128 * h + 128] * scale_q + qpad[h : h + 1, :]
            ).astype(BF16)
        for h in range(2):
            at = 512 + 256 * h
            stg[t, h, 2, span, :] = (result[:, at : at + 128] * scale + flag).astype(BF16)
            stg[t, h, 3, span, :] = (result[:, at + 128 : at + 256] * scale + ones_lane).astype(BF16)
        q_exchange(t, r).start()

    for r in range(XN):
        norm(0, r)
    for n in ready:
        prepare(n)

    def a_exchange(t, r):
        return remote(asend.at[t, r], arecv.at[t, r], asm.at[t, r], arm.at[t, r], sib)

    def attend(t, r):
        keys = jnp.concatenate([stg[t, c, 2], rcv[t, 2]], axis=0)
        values = jnp.concatenate([stg[t, c, 3], rcv[t, 3]], axis=0)
        scores = []
        for h in range(2):
            scores.append(dot_nt(stg[t, c, h, rows(r), :], keys))
            scores.append(dot_nt(rcv[t, h, rows(r), :], keys))
        powers = [jnp.exp2(each - jnp.max(each, axis=1, keepdims=True)).astype(BF16) for each in scores]
        for n, each in enumerate(powers):
            total = dot(each, values)
            result = (total * (1.0 / total[:, HEAD : HEAD + 1])).astype(BF16)
            if n % 2 == 0:
                atto[r, n // 2] = result
            else:
                asend[t, r, n // 2] = result
        a_exchange(t, r).start()

    def finish(t, r):
        a_exchange(t, r).wait_recv()
        heads = jnp.concatenate([atto[r, 0], atto[r, 1], arecv[t, r, 0], arecv[t, r, 1]], axis=1)
        attended = dot(heads, psel[...])
        hidden = xg[t, rows(r), cols(x)].astype(F32) + dot_t(
            onehot(contact_rows(t, r)), table[0, :, cols(x)]
        )
        ob[t, r] = (hidden + gate[:, cols(x)] * attended).astype(BF16)
        if t + 1 < TURNS:
            @pl.when(s < SN - 1)
            def _():
                y_copy(t, r).start()

    def out_copy(t, d):
        return remote(
            ob.at[t, xat(d)], out.at[0, t, 0, :, cols(x)], osm.at[t, d], orm.at[t, d], xdev(d)
        )

    def out_arrival(t, d):
        return remote(
            ob.at[t, xat(d)], out.at[0, t, 0, :, cols(xat(-d))], osm.at[t, d], orm.at[t, d], xdev(d)
        )

    def out_own(t):
        return pltpu.make_async_copy(ob.at[t, x], out.at[0, t, 0, :, cols(x)], osm.at[t, 0])

    for t in range(TURNS):
        if t == 0:
            for r in range(XN):
                project(t, r)
        else:
            x_start(t, 2)
            x_forward(t, 0)
            x_start(t, 3)
            x_forward(t, 1)
            x_forward(t, 2)
            x_forward(t, 3)
            for a in range(XN):
                if a == 0:
                    x_finish(t, 0)

                    @pl.when(s == 0)
                    def _(t=t):
                        for later in range(1, XN):
                            x_finish(t, later)
                else:
                    @pl.when(s > 0)
                    def _(t=t, a=a):
                        x_finish(t, a)

                norm(t, a)
                project(t, a)
            out_own(t - 1).start()
            for d in (2, 1, 3):
                out_copy(t - 1, d).start()
        for r in range(XN):
            q_exchange(t, r).wait_recv()

        def step(n, _, t=t):
            attend(t, n if t + 1 < TURNS else xat(n + 1))

            @pl.when(n > 0)
            def _():
                if t + 1 < TURNS:
                    finish(t, n - 1)
                else:
                    finish(t, xat(n))
                    out_copy(t, n).start()

            return 0

        lax.fori_loop(0, XN, step, 0)
        if t + 1 < TURNS:
            x_start(t + 1, 0)
            finish(t, XN - 1)
            x_start(t + 1, 1)
        else:
            finish(t, x)
            out_own(t).start()
        if t == 0:
            for n in range(TURNS):
                for d in (1, 2, 3):
                    cot_piece(n, d, xat(-d)).wait_recv()
        share = dot_t(ob[t].reshape(XN * B, CW), cotv[:, t].reshape(XN * B, 256))
        gacc[...] = share if t == 0 else gacc[...] + share

    g_sib = remote(
        gacc.at[pl.ds(pl.multiple_of((1 - c) * 192, 64), 192)], grec, gs.at[0], gr.at[0], sib
    )
    g_sib.start()
    g_sib.wait_recv()
    gsum[...] = gacc[pl.ds(pl.multiple_of(c * 192, 64), 192), :] + grec[...]
    gpass[...] = gsum[...].reshape(ZN, 24, 256).astype(BF16)

    def g_copy(d):
        return remote(
            gpass.at[zat(d)], grz.at[d - 1], gs.at[d], gr.at[d], zdev(d)
        )

    for d in (4, 3, 5, 2, 6, 1, 7):
        g_copy(d).start()
    total = gsum[pl.ds(pl.multiple_of(24 * j, 8), 24), :]
    for d in (1, 7, 2, 6, 3, 5, 4):
        g_copy(d).wait_recv()
        total = total + grz[d - 1].astype(F32)
    grad[0] = total * (float(TURNS * ZN * 1024) ** (-0.5))

    for d in (1, 2, 3):
        for n, w in enumerate((wq, wkv)):
            w_piece(d, n, w).wait_send()
        ct_piece(d, x).wait_send()
    for n in range(XN):
        for k in range(half + 1):
            for way in range(2):
                if k > 0:
                    z_send(n, k, way).wait_send()
                if k > 0 or way == 0:
                    sib_send(c, n, k, way).wait_send()
    for t in range(TURNS):
        out_own(t).wait()
        for d in (1, 2, 3):
            cot_piece(t, d, x).wait_send()
            out_copy(t, d).wait_send()
            out_arrival(t, d).wait_recv()
        for a in range(XN):
            x_send(t, a, 0).wait_send()
            x_send(t, a, 1).wait_send()
            x_pass(t, a).wait_send()
            a_exchange(t, a).wait_send()
            q_exchange(t, a).wait_send()
    @pl.when(s < SN - 1)
    def _():
        for t in range(TURNS - 1):
            for a in range(XN):
                y_copy(t, a).wait_send()

    g_sib.wait_send()
    for d in range(1, ZN):
        g_copy(d).wait_send()


def body(*args):
    args = list(args)
    args[3] = args[3].reshape(1, args[3].shape[0])
    vmem = pl.BlockSpec(memory_space=pltpu.VMEM)
    smem = pl.BlockSpec(memory_space=pltpu.SMEM)
    anys = pl.BlockSpec(memory_space=pl.ANY)
    dma = pltpu.SemaphoreType.DMA
    return pl.pallas_call(
        kernel,
        out_shape=(
            pltpu.VMEM((1, TURNS, 1, B, D), BF16),
            pltpu.VMEM((1, 24, 256), F32),
        ),
        in_specs=[anys, anys, vmem, smem, anys, anys, vmem, vmem, vmem, vmem, vmem, anys],
        out_specs=(vmem, vmem),
        scratch_shapes=[
            pltpu.VMEM((TURNS, 4 * B, D), BF16),
            pltpu.VMEM((2, ZN, XN, 24, 2 * CW), BF16),
            pltpu.VMEM((D, 1024), BF16),
            pltpu.VMEM((XN, 10, 1, B), jnp.int32),
            pltpu.VMEM((XN, TURNS, B, 256), BF16),
            pltpu.VMEM((TURNS, 2, 4, 4 * B, 128), BF16),
            pltpu.VMEM((TURNS, 4, 4 * B, 128), BF16),
            pltpu.VMEM((4 * B, D), BF16),
            pltpu.VMEM((4 * B, 128), F32),
            pltpu.VMEM((TURNS, XN, 2, B, 128), BF16),
            pltpu.VMEM((TURNS, XN, 2, B, 128), BF16),
            pltpu.VMEM((XN, 2, B, 128), BF16),
            pltpu.VMEM((TURNS, XN, B, CW), BF16),
            pltpu.VMEM((8, D), F32),
            pltpu.VMEM((512, CW), BF16),
            pltpu.VMEM((CW, 512), BF16),
            pltpu.VMEM((8, 128), F32),
            pltpu.VMEM((CW, 256), F32),
            pltpu.VMEM((192, 256), F32),
            pltpu.VMEM((192, 256), F32),
            pltpu.VMEM((ZN, 24, 256), BF16),
            pltpu.VMEM((ZN - 1, 24, 256), BF16),
            dma((TURNS, XN, 3)),
            dma((TURNS, XN, 3)),
            dma((4,)),
            dma((TURNS - 1, XN)),
            dma((TURNS - 1, XN)),
            dma((3, 2)),
            dma((3, 2)),
            dma((2,)),
            dma((XN, 4, 2)),
            dma((XN, 4, 2)),
            dma((XN, 5, 2)),
            dma((XN, 5, 2)),
            dma((4,)),
            dma((4,)),
            dma((TURNS, 3)),
            dma((TURNS, 3)),
            dma((TURNS, XN)),
            dma((TURNS, XN)),
            dma((TURNS, XN)),
            dma((TURNS, XN)),
            dma((TURNS, XN)),
            dma((TURNS, XN)),
            dma((ZN,)),
            dma((ZN,)),
        ],
        compiler_params=pltpu.CompilerParams(
            collective_id=0, has_side_effects=True, vmem_limit_bytes=56 * 1024 * 1024
        ),
        cost_estimate=pl.CostEstimate(
            flops=10_000_000_000, bytes_accessed=16_000_000, transcendentals=7_000_000
        ),
    )(*args)


def solution(mesh):
    in_specs = (
        P("pipe", None, "dp", "seq", None),
        P(None, "dp", "seq"),
        P(None, "dp", None),
        P(None, "dp"),
        P("pipe", ("seq", "dp"), None),
        P("pipe", ("seq", "dp"), None),
        P("pipe", None),
        P("pipe", None),
        P("pipe", None, None),
        P("pipe", None),
        P("pipe", None),
        P("pipe", None, "dp", "seq", None),
    )
    out_specs = (P("pipe", None, "dp", "seq", None), P("pipe", ("seq", "dp"), None))
    return jax.shard_map(body, mesh=mesh, in_specs=in_specs, out_specs=out_specs, check_vma=False)
```

```python
import functools
import math

import jax
import jax.numpy as jnp
from jax import lax
from jax.experimental import pallas as pl
from jax.experimental.pallas import tpu as pltpu
from jax.sharding import PartitionSpec as P

BF16 = jnp.bfloat16
F32 = jnp.float32
MESH = pl.DeviceIdType.MESH
EPSILON = 1e-06
LOG2E = math.log2(math.e)
XN = 4
ZN = 8
SN = 8
TURNS = 3
ORDER = (0, 1, 3, 2)
SKEW = 3
FORWARD_AT = (4, 7, 10, 13)
D = 1536
CW = 384
HEAD = 96
B = 128


def dot(a, b):
    return jnp.dot(a, b, preferred_element_type=F32)


def dot_t(a, b):
    return lax.dot_general(a, b, (((0,), (0,)), ((), ())), preferred_element_type=F32)


def dot_nt(a, b):
    return lax.dot_general(a, b, (((1,), (1,)), ((), ())), preferred_element_type=F32)


def kernel(
    inc, contacts, keyframes, timesteps, wq, wkv, gain, freq, table, kbias, gate, cot,
    out, grad,
    xg, wr, wp, ctv, cotv, stg, rcv, act, scales, asend, arecv, atto, ob, modv, psel, pw, qpad, gacc, grec, gsum, gpass, grz,
    xs, xrv, lx, ys, yr, ws, wrv, wl, zs, zr, bs, br, cs, cr, ks, kr, qs, qr, asm, arm, osm, orm, gs, gr,
):
    s = lax.axis_index("pipe")
    i = lax.axis_index("seq")
    j = lax.axis_index("dp")
    x = lax.div(i, 2)
    c = lax.rem(i, 2)
    first = lax.div(SN - s, SN)

    def xat(d):
        return lax.rem(x + d + XN, XN)

    def zat(d):
        return lax.rem(j + d + ZN, ZN)

    def xdev(d):
        return (s, 2 * xat(d) + c, j)

    def zdev(d):
        return (s, i, zat(d))

    sib = (s, 2 * x + 1 - c, j)
    ynext = (lax.rem(s + 1, SN), i, j)
    yprev = (lax.rem(s + SN - 1, SN), i, j)

    def remote(src, dst, send, recv, device):
        return pltpu.make_async_remote_copy(
            src_ref=src, dst_ref=dst, send_sem=send, recv_sem=recv, device_id=device, device_id_type=MESH
        )

    def cols(b):
        return pl.ds(pl.multiple_of(b * CW, 128), CW)

    def rows(r):
        return pl.ds(pl.multiple_of(r * B, B), B)

    barrier = pltpu.get_barrier_semaphore()
    peers = [xdev(1), xdev(2), xdev(3), sib, ynext, yprev] + [zdev(d) for d in range(1, ZN)]
    for peer in peers:
        pl.semaphore_signal(barrier, inc=1, device_id=peer, device_id_type=MESH)

    own_x0 = pltpu.make_async_copy(inc.at[0, 0, 0], xg.at[0, rows(x)], lx.at[0])
    own_x0.start()
    own_ct = pltpu.make_async_copy(contacts, ctv.at[x], cs.at[0])
    own_ct.start()
    own_cot = pltpu.make_async_copy(cot.at[0, :, 0], cotv.at[x], lx.at[3])
    own_cot.start()
    own_w = [
        pltpu.make_async_copy(w.at[0, :, cols(x)], wr.at[c, j, x, :, CW * n : CW * n + CW], wl.at[n])
        for n, w in enumerate((wq, wkv))
    ]
    for copy in own_w:
        copy.start()

    def own_later(t):
        return pltpu.make_async_copy(inc.at[0, t, 0], xg.at[t, rows(x)], lx.at[t])

    @pl.when(s == 0)
    def _():
        own_later(1).start()
        own_later(2).start()

    pl.semaphore_wait(barrier, len(peers))

    def w_piece(d, n, w):
        return remote(
            w.at[0, :, cols(xat(d))],
            wr.at[c, j, x, :, CW * n : CW * n + CW],
            ws.at[d - 1, n],
            wrv.at[d - 1, n],
            xdev(d),
        )

    def w_arrival(d, n):
        here = wr.at[c, j, xat(-d), :, CW * n : CW * n + CW]
        return remote(here, here, ws.at[d - 1, n], wrv.at[d - 1, n], xdev(d))

    for d in (1, 3, 2):
        for n, w in enumerate((wq, wkv)):
            w_piece(d, n, w).start()

    def ct_piece(d, src):
        return remote(ctv.at[src], ctv.at[src], cs.at[d], cr.at[d], xdev(d))

    def cot_piece(t, d, src):
        return remote(cotv.at[src, t], cotv.at[src, t], ks.at[t, d - 1], kr.at[t, d - 1], xdev(d))

    def piece(t, a, b):
        if t == 0:
            r, n = b, a
        else:
            r, n = a + first * (b - a), b + first * (a - b)
        return xg.at[t, rows(r), cols(n)]

    def x_send(t, a, way):
        dst = piece(t, a, x)
        src = inc.at[0, 0, 0, :, CW * a : CW * a + CW] if t == 0 else dst
        return remote(src, dst, xs.at[t, a, way], xrv.at[t, a, way], xdev(1 - 2 * way))

    def x_arrival(t, a, way):
        here = piece(t, a, xat(2 * way - 1))
        return remote(here, here, xs.at[t, a, way], xrv.at[t, a, way], xdev(1))

    def x_pass(t, a):
        way = a % 2
        here = piece(t, a, xat(2 * way - 1))
        return remote(here, here, xs.at[t, a, 2], xrv.at[t, a, 2], xdev(1 - 2 * way))

    def x_passed(t, a):
        here = piece(t, a, xat(2))
        return remote(here, here, xs.at[t, a, 2], xrv.at[t, a, 2], xdev(1))

    def y_copy(t, r):
        return remote(ob.at[t, r], xg.at[t + 1, rows(r), cols(x)], ys.at[t, r], yr.at[t, r], ynext)

    def x_start(t, a):
        if t > 0:
            @pl.when(s > 0)
            def _():
                y_copy(t - 1, a).wait_recv()

            if a == 0:
                @pl.when(s == 0)
                def _():
                    own_later(t).wait()

        x_send(t, a, 0).start()
        x_send(t, a, 1).start()

    def x_forward(t, a):
        x_arrival(t, a, a % 2).wait_recv()
        x_pass(t, a).start()

    def x_finish(t, a):
        x_arrival(t, a, 1 - a % 2).wait_recv()
        x_passed(t, a).wait_recv()

    for a in range(XN):
        x_start(0, a)
    own_ct.wait()
    for d in (1, 2, 3):
        ct_piece(d, x).start()

    lane = lax.broadcasted_iota(jnp.int32, (1, 128), 1)
    head_lane = lax.broadcasted_iota(jnp.int32, (1, 16), 1)
    for h in range(4):
        b = jnp.sum(jnp.where(head_lane == 4 * x + h, kbias[...], 0.0), axis=1, keepdims=True) * LOG2E
        high = b.astype(BF16).astype(F32)
        qpad[h : h + 1, :] = jnp.where(lane == HEAD, high, 0.0) + jnp.where(lane == HEAD + 1, b - high, 0.0)
    for t in range(TURNS):
        step = timesteps[0, t - s + SN - 1].astype(F32)
        modv[t : t + 1, :] = gain[...] * (1.0 + 0.5 * jnp.sin(step * freq[...]))
    row = lax.broadcasted_iota(jnp.int32, (512, CW), 0)
    col = lax.broadcasted_iota(jnp.int32, (512, CW), 1)
    slot = lax.shift_right_logical(row, 7)
    low = row - slot * 128
    head = jnp.where(slot < 2, slot + 2 * c, slot - 2 * c)
    psel[...] = jnp.where((low < HEAD) & (col == head * HEAD + low), 1.0, 0.0).astype(BF16)
    row = lax.broadcasted_iota(jnp.int32, (CW, 512), 0)
    col = lax.broadcasted_iota(jnp.int32, (CW, 512), 1)
    slot = lax.shift_right_logical(col, 7)
    low = col - slot * 128
    pw[...] = jnp.where((low < HEAD) & (row == slot * HEAD + low), 1.0, 0.0).astype(BF16)

    half = ZN // 2

    def part(core, xx, zz, k, way):
        block = wr.at[core, zz, xx]
        return block if k < half else block.at[:, pl.ds(CW * way, CW)]

    def came(k, way):
        return zat(-k) if way == 0 else zat(k)

    def z_send(n, k, way):
        ref = part(c, xat(ORDER[n]), zat(1 - k) if way == 0 else zat(k - 1), k, way)
        return remote(ref, ref, zs.at[n, k - 1, way], zr.at[n, k - 1, way], zdev(1 - 2 * way))

    def z_arrival(n, k, way):
        ref = part(c, xat(ORDER[n]), came(k, way), k, way)
        return remote(ref, ref, zs.at[n, k - 1, way], zr.at[n, k - 1, way], zdev(1))

    def sib_send(core, n, k, way):
        ref = part(core, xat(ORDER[n]), came(k, way), k, way)
        return remote(ref, ref, bs.at[n, k, way], br.at[n, k, way], sib)

    def z_step(n, k):
        if k == 0:
            if n == 0:
                for copy in own_w:
                    copy.wait()
            else:
                w_arrival((XN - ORDER[n]) % XN, 0).wait_recv()
                w_arrival((XN - ORDER[n]) % XN, 1).wait_recv()
            z_send(n, 1, 0).start()
            z_send(n, 1, 1).start()
            sib_send(c, n, 0, 0).start()
            return
        for way in range(2):
            z_arrival(n, k, way).wait_recv()
            if k < half:
                z_send(n, k + 1, way).start()
            sib_send(c, n, k, way).start()

    def prepare(n):
        sib_send(1 - c, n, 0, 0).wait_recv()
        for k in range(1, half + 1):
            for way in range(2):
                sib_send(1 - c, n, k, way).wait_recv()
        xx = xat(ORDER[n])

        def one(cc, _):
            block = wr[cc, :, xx].astype(F32).reshape(ZN * 24, 2 * CW).astype(BF16)
            dst = pl.ds(pl.multiple_of((2 * xx + cc) * 192, 64), 192)
            wp[dst, 0:512] = dot(block[:, :CW], pw[...]).astype(BF16)
            wp[dst, 512:1024] = dot(block[:, CW:], pw[...]).astype(BF16)
            return 0

        lax.fori_loop(0, 2, one, 0)

    steps = sorted((SKEW * k + n, n, k) for n in range(XN) for k in range(half + 1))
    ready = []
    for at, (_, n, k) in enumerate(steps):
        z_step(n, k)
        if at in FORWARD_AT:
            x_forward(0, FORWARD_AT.index(at))
        if ready:
            prepare(ready.pop())
        if k == half:
            ready.append(n)
    own_x0.wait()
    own_cot.wait()
    for a in range(XN):
        x_finish(0, a)
    for t in range(TURNS):
        for d in (1, 2, 3):
            cot_piece(t, d, x).start()
    for d in (1, 2, 3):
        ct_piece(d, xat(-d)).wait_recv()

    def contact_rows(t, r):
        return ctv[r, t - s + SN - 1]

    def onehot(values):
        count = values.shape[1]
        states = lax.broadcasted_iota(jnp.int32, (16, count), 0)
        return jnp.where(states == values, 1.0, 0.0).astype(BF16)

    place = lax.broadcasted_iota(jnp.int32, (16, 128), 0)
    place_lane = lax.broadcasted_iota(jnp.int32, (16, 128), 1)
    flag_lanes = jnp.where(
        (place == 0) & ((place_lane == HEAD) | (place_lane == HEAD + 1)), 1.0, 0.0
    ).astype(BF16)
    ones_lane = jnp.where(lane == HEAD, 1.0, 0.0)

    def q_exchange(t, r):
        span = pl.ds(B * r, B)
        return remote(stg.at[t, 1 - c, :, span], rcv.at[t, :, span], qs.at[t, r], qr.at[t, r], sib)

    def norm(t, r):
        span = slice(B * r, B * r + B)
        hidden = xg[t, span, :].astype(F32) + dot_t(onehot(contact_rows(t, r)), table[0])
        square = jnp.sum(hidden * hidden, axis=1, keepdims=True)
        act[span, :] = (hidden * modv[t : t + 1, :]).astype(BF16)
        scales[span, :] = jnp.broadcast_to(lax.rsqrt(square * (1.0 / D) + EPSILON), (B, 128))

    def project(t, r):
        span = slice(B * r, B * r + B)
        scale = scales[span, :]
        flag = keyframes[t - s + SN - 1, :, pl.ds(pl.multiple_of((2 * r + c) * B, B), B)]
        flag = dot_t(jnp.where(place == 0, flag.astype(F32), 0.0).astype(BF16), flag_lanes)
        result = dot(act[span, :], wp[...])
        scale_q = scale * (LOG2E * HEAD ** (-0.5))
        for h in range(4):
            stg[t, h // 2, h % 2, span, :] = (
                result[:, 128 * h : 128 * h + 128] * scale_q + qpad[h : h + 1, :]
            ).astype(BF16)
        for h in range(2):
            at = 512 + 256 * h
            stg[t, h, 2, span, :] = (result[:, at : at + 128] * scale + flag).astype(BF16)
            stg[t, h, 3, span, :] = (result[:, at + 128 : at + 256] * scale + ones_lane).astype(BF16)
        q_exchange(t, r).start()

    for r in range(XN):
        norm(0, r)
    for n in ready:
        prepare(n)

    def a_exchange(t, r):
        return remote(asend.at[t, r], arecv.at[t, r], asm.at[t, r], arm.at[t, r], sib)

    def attend(t, r):
        keys = jnp.concatenate([stg[t, c, 2], rcv[t, 2]], axis=0)
        values = jnp.concatenate([stg[t, c, 3], rcv[t, 3]], axis=0)
        scores = []
        for h in range(2):
            scores.append(dot_nt(stg[t, c, h, rows(r), :], keys))
            scores.append(dot_nt(rcv[t, h, rows(r), :], keys))
        powers = [jnp.exp2(each - jnp.max(each, axis=1, keepdims=True)).astype(BF16) for each in scores]
        for n, each in enumerate(powers):
            total = dot(each, values)
            result = (total * (1.0 / total[:, HEAD : HEAD + 1])).astype(BF16)
            if n % 2 == 0:
                atto[r, n // 2] = result
            else:
                asend[t, r, n // 2] = result
        a_exchange(t, r).start()

    def finish(t, r):
        a_exchange(t, r).wait_recv()
        heads = jnp.concatenate([atto[r, 0], atto[r, 1], arecv[t, r, 0], arecv[t, r, 1]], axis=1)
        attended = dot(heads, psel[...])
        hidden = xg[t, rows(r), cols(x)].astype(F32) + dot_t(
            onehot(contact_rows(t, r)), table[0, :, cols(x)]
        )
        ob[t, r] = (hidden + gate[:, cols(x)] * attended).astype(BF16)
        if t + 1 < TURNS:
            @pl.when(s < SN - 1)
            def _():
                y_copy(t, r).start()

    def out_copy(t, d):
        return remote(
            ob.at[t, xat(d)], out.at[0, t, 0, :, cols(x)], osm.at[t, d], orm.at[t, d], xdev(d)
        )

    def out_arrival(t, d):
        return remote(
            ob.at[t, xat(d)], out.at[0, t, 0, :, cols(xat(-d))], osm.at[t, d], orm.at[t, d], xdev(d)
        )

    def out_own(t):
        return pltpu.make_async_copy(ob.at[t, x], out.at[0, t, 0, :, cols(x)], osm.at[t, 0])

    for t in range(TURNS):
        if t == 0:
            for r in range(XN):
                project(t, r)
        else:
            x_start(t, 2)
            x_forward(t, 0)
            x_start(t, 3)
            x_forward(t, 1)
            x_forward(t, 2)
            x_forward(t, 3)
            for a in range(XN):
                if a == 0:
                    x_finish(t, 0)

                    @pl.when(s == 0)
                    def _(t=t):
                        for later in range(1, XN):
                            x_finish(t, later)
                else:
                    @pl.when(s > 0)
                    def _(t=t, a=a):
                        x_finish(t, a)

                norm(t, a)
                project(t, a)
            out_own(t - 1).start()
            for d in (2, 1, 3):
                out_copy(t - 1, d).start()
        for r in range(XN):
            q_exchange(t, r).wait_recv()

        for n in range(XN):
            attend(t, n if t + 1 < TURNS else xat(n + 1))
            if n > 0:
                if t + 1 < TURNS:
                    finish(t, n - 1)
                else:
                    finish(t, xat(n))
                    out_copy(t, n).start()
        if t + 1 < TURNS:
            x_start(t + 1, 0)
            finish(t, XN - 1)
            x_start(t + 1, 1)
        else:
            finish(t, x)
            out_own(t).start()
        if t == 0:
            for n in range(TURNS):
                for d in (1, 2, 3):
                    cot_piece(n, d, xat(-d)).wait_recv()
        share = dot_t(ob[t].reshape(XN * B, CW), cotv[:, t].reshape(XN * B, 256))
        gacc[...] = share if t == 0 else gacc[...] + share

    g_sib = remote(
        gacc.at[pl.ds(pl.multiple_of((1 - c) * 192, 64), 192)], grec, gs.at[0], gr.at[0], sib
    )
    g_sib.start()
    g_sib.wait_recv()
    gsum[...] = gacc[pl.ds(pl.multiple_of(c * 192, 64), 192), :] + grec[...]
    gpass[...] = gsum[...].reshape(ZN, 24, 256).astype(BF16)

    def g_copy(d):
        return remote(
            gpass.at[zat(d)], grz.at[d - 1], gs.at[d], gr.at[d], zdev(d)
        )

    for d in (4, 3, 5, 2, 6, 1, 7):
        g_copy(d).start()
    total = gsum[pl.ds(pl.multiple_of(24 * j, 8), 24), :]
    for d in (1, 7, 2, 6, 3, 5, 4):
        g_copy(d).wait_recv()
        total = total + grz[d - 1].astype(F32)
    grad[0] = total * (float(TURNS * ZN * 1024) ** (-0.5))

    for d in (1, 2, 3):
        for n, w in enumerate((wq, wkv)):
            w_piece(d, n, w).wait_send()
        ct_piece(d, x).wait_send()
    for n in range(XN):
        for k in range(half + 1):
            for way in range(2):
                if k > 0:
                    z_send(n, k, way).wait_send()
                if k > 0 or way == 0:
                    sib_send(c, n, k, way).wait_send()
    for t in range(TURNS):
        out_own(t).wait()
        for d in (1, 2, 3):
            cot_piece(t, d, x).wait_send()
            out_copy(t, d).wait_send()
            out_arrival(t, d).wait_recv()
        for a in range(XN):
            x_send(t, a, 0).wait_send()
            x_send(t, a, 1).wait_send()
            x_pass(t, a).wait_send()
            a_exchange(t, a).wait_send()
            q_exchange(t, a).wait_send()
    @pl.when(s < SN - 1)
    def _():
        for t in range(TURNS - 1):
            for a in range(XN):
                y_copy(t, a).wait_send()

    g_sib.wait_send()
    for d in range(1, ZN):
        g_copy(d).wait_send()


def body(*args):
    args = list(args)
    args[3] = args[3].reshape(1, args[3].shape[0])
    vmem = pl.BlockSpec(memory_space=pltpu.VMEM)
    smem = pl.BlockSpec(memory_space=pltpu.SMEM)
    anys = pl.BlockSpec(memory_space=pl.ANY)
    dma = pltpu.SemaphoreType.DMA
    return pl.pallas_call(
        kernel,
        out_shape=(
            pltpu.VMEM((1, TURNS, 1, B, D), BF16),
            pltpu.VMEM((1, 24, 256), F32),
        ),
        in_specs=[anys, anys, vmem, smem, anys, anys, vmem, vmem, vmem, vmem, vmem, anys],
        out_specs=(vmem, vmem),
        scratch_shapes=[
            pltpu.VMEM((TURNS, 4 * B, D), BF16),
            pltpu.VMEM((2, ZN, XN, 24, 2 * CW), BF16),
            pltpu.VMEM((D, 1024), BF16),
            pltpu.VMEM((XN, 10, 1, B), jnp.int32),
            pltpu.VMEM((XN, TURNS, B, 256), BF16),
            pltpu.VMEM((TURNS, 2, 4, 4 * B, 128), BF16),
            pltpu.VMEM((TURNS, 4, 4 * B, 128), BF16),
            pltpu.VMEM((4 * B, D), BF16),
            pltpu.VMEM((4 * B, 128), F32),
            pltpu.VMEM((TURNS, XN, 2, B, 128), BF16),
            pltpu.VMEM((TURNS, XN, 2, B, 128), BF16),
            pltpu.VMEM((XN, 2, B, 128), BF16),
            pltpu.VMEM((TURNS, XN, B, CW), BF16),
            pltpu.VMEM((8, D), F32),
            pltpu.VMEM((512, CW), BF16),
            pltpu.VMEM((CW, 512), BF16),
            pltpu.VMEM((8, 128), F32),
            pltpu.VMEM((CW, 256), F32),
            pltpu.VMEM((192, 256), F32),
            pltpu.VMEM((192, 256), F32),
            pltpu.VMEM((ZN, 24, 256), BF16),
            pltpu.VMEM((ZN - 1, 24, 256), BF16),
            dma((TURNS, XN, 3)),
            dma((TURNS, XN, 3)),
            dma((4,)),
            dma((TURNS - 1, XN)),
            dma((TURNS - 1, XN)),
            dma((3, 2)),
            dma((3, 2)),
            dma((2,)),
            dma((XN, 4, 2)),
            dma((XN, 4, 2)),
            dma((XN, 5, 2)),
            dma((XN, 5, 2)),
            dma((4,)),
            dma((4,)),
            dma((TURNS, 3)),
            dma((TURNS, 3)),
            dma((TURNS, XN)),
            dma((TURNS, XN)),
            dma((TURNS, XN)),
            dma((TURNS, XN)),
            dma((TURNS, XN)),
            dma((TURNS, XN)),
            dma((ZN,)),
            dma((ZN,)),
        ],
        compiler_params=pltpu.CompilerParams(
            collective_id=0, has_side_effects=True, vmem_limit_bytes=56 * 1024 * 1024
        ),
        cost_estimate=pl.CostEstimate(
            flops=10_000_000_000, bytes_accessed=16_000_000, transcendentals=7_000_000
        ),
    )(*args)


def solution(mesh):
    in_specs = (
        P("pipe", None, "dp", "seq", None),
        P(None, "dp", "seq"),
        P(None, "dp", None),
        P(None, "dp"),
        P("pipe", ("seq", "dp"), None),
        P("pipe", ("seq", "dp"), None),
        P("pipe", None),
        P("pipe", None),
        P("pipe", None, None),
        P("pipe", None),
        P("pipe", None),
        P("pipe", None, "dp", "seq", None),
    )
    out_specs = (P("pipe", None, "dp", "seq", None), P("pipe", ("seq", "dp"), None))
    return jax.shard_map(body, mesh=mesh, in_specs=in_specs, out_specs=out_specs, check_vma=False)
```
